512 devices in a mesh: env: 64 (over z_lo, x, core), sp: 8 (over y, z_hi).
Axes of the slice: x: 4, y: 4, z: 16 (z_hi: 2, z_lo: 8; z = z_hi * 8 + z_lo), core: 2. Of those that a mesh axis runs over, the one named last changes fastest.
Arguments:
- descriptors: bfloat16 [98304, 1024], P('env'), may hold values from -6 to 6
- env_species: int32 [98304], P('env'), may hold values from 0 to 3
- structure: int32 [64, 1536], P('env'), may hold values from 0 to 23, never falling along the last dimension, each value on 1 to 128 neighbouring positions
- energies: float32 [1536], P('env'), may hold values from -6 to 6
- sparse_points: bfloat16 [4096, 1024], P('sp'), may hold values from -6 to 6
- sparse_species: int32 [4096], P('sp'), may hold values from 0 to 3
Outputs:
- gram: float32 [4096, 4096], P('sp', 'env')
- fit_rhs: float32 [4096], P('sp')
The draws below stay inside these ranges and needn't reach their ends.
Inputs may be any that keep to these rules, and one draw needn't show every extreme that they name: Each row numbers the structures of one index of env from 0 to 23 in order, never falling; each structure has 1 to 128 environments and some has exactly 128.
All inputs are finite; a program needn't handle non-finite values.
Results may differ from the reference program's by a relative error of at most 0.0003.
Values sent between devices are 32-bit elements; how exact they have to be, the bound alone decides.
No kernel may reach another device: no remote copies, remote signals or barrier semaphores. Data moves between devices by JAX's collectives and lax.ppermute only.
A program may use at most 64 MiB of HBM per device.

```python
import math
import jax
import jax.numpy as jnp
import numpy as np
from jax import lax

D = 1024
M = 4096
ENV_DEV = 1536
STR_DEV = 24
ATOMS_MOST = 128
SPECIES = 4
ENVS = 98304
STRUCTS = 1536
N_ENV = 64


def set_ends(drawn, stream_key, least, top_value):
    longest = drawn.shape.index(max(drawn.shape))
    spots = []
    for shift in (0, 1):
        where = [jax.random.randint(jax.random.fold_in(stream_key, axis), (), 0, length) for axis, length in enumerate(drawn.shape)]
        where[longest] = (where[longest] + shift) % drawn.shape[longest]
        spots.append(tuple(where))
    return drawn.at[spots[0]].set(least).at[spots[1]].set(top_value)


def levels(key, dims, shards, smallest, largest):
    def one(position, shards_of):
        heights = jax.random.uniform(jax.random.fold_in(jax.random.fold_in(key, 6), position), (shards_of,), jnp.float32, smallest / len(shards), largest / len(shards))
        return jnp.repeat(jnp.exp(heights), dims[position] // shards_of).reshape((-1,) + (1,) * (len(dims) - position - 1))

    gain = one(*shards[0])
    for cut in shards[1:]:
        gain = gain * one(*cut)
    return gain


def cumulative_ranks(amount, lean):
    weights = [(1 << 20) // math.isqrt(grade ** lean) + 1 for grade in range(1, amount + 1)]
    width = 1 + sum(weights) // (1 << 30)
    return np.cumsum(np.array([max(1, weight // width) for weight in weights]))


def skewed_ids(key, dims, number_of, slope):
    listing = cumulative_ranks(number_of, slope)
    lot = jax.random.randint(jax.random.fold_in(key, 1), dims, 0, int(listing[number_of - 1]))
    grade = jnp.searchsorted(jnp.asarray(listing, jnp.int32), lot, side="right")
    return jax.random.permutation(jax.random.fold_in(key, 2), number_of)[grade].astype(jnp.int32)


def split_up(count, total, most, skew):
    portions = [(1 << 20) // math.isqrt(grade ** skew) + 1 for grade in range(2, count + 1)]
    rest, given = total - most - (count - 1), [1] * (count - 1)
    while rest > 0:
        candidates = [i for i in range(count - 1) if given[i] < most]
        mass, left = sum([portions[i] for i in candidates]), rest
        for i in candidates:
            addition = min(most - given[i], max(1, left * portions[i] // mass), rest)
            given[i] = given[i] + addition
            rest = rest - addition
    return np.array([most] + given)


def ragged_sizes(own_key, number_of, total, bound, skew):
    if number_of == 2:
        one = jax.random.randint(own_key, (), max(1, total - bound), min(bound, total - 1) + 1)
        return jnp.stack([one, total - one])
    lengths = jnp.asarray(split_up(number_of, total, bound, skew), jnp.int32)
    twos = (number_of - 1) // 2
    source_of, sink = lengths[1:1 + 2 * twos:2], lengths[2:2 + 2 * twos:2]
    room = jnp.minimum(source_of - 1, bound - sink)
    passed = jax.random.randint(jax.random.fold_in(own_key, 1), (twos,), 0, 1 << 20) % (room + 1)
    lengths = lengths.at[1:1 + 2 * twos:2].set(source_of - passed).at[2:2 + 2 * twos:2].set(sink + passed)
    return lengths[jax.random.permutation(jax.random.fold_in(own_key, 2), number_of)]


def noise(own_key, shape, deviation, most, shards=(), held_as=jnp.bfloat16):
    factor_of = levels(own_key, shape, shards, -0.22, 0.18) if shards else 1.0
    entries = jax.random.normal(own_key, shape, jnp.float32) * deviation * factor_of
    return jnp.minimum(jnp.maximum(entries, -most), most).astype(held_as)


def setup_inputs(seed: int = 0) -> dict:
    arg_keys = jax.random.split(jax.random.key(seed), 7)
    return {
        "descriptors": noise(arg_keys[0], (ENVS, D), 1.0, 6.0, ((0, 64),)),
        "env_species": set_ends(skewed_ids(arg_keys[1], (ENVS,), SPECIES, 2), jax.random.fold_in(arg_keys[1], 3), 0, SPECIES - 1).astype(jnp.int32),
        "structure": jax.vmap(lambda own: jnp.searchsorted(jnp.cumsum(ragged_sizes(own, STR_DEV, ENV_DEV, ATOMS_MOST, 1)), jnp.arange(ENV_DEV), side="right"))(jax.random.split(arg_keys[2], N_ENV)).reshape((N_ENV, ENV_DEV)).astype(jnp.int32),
        "energies": noise(arg_keys[3], (STRUCTS,), 1.0, 6.0, ((0, 64),), jnp.float32),
        "sparse_points": noise(arg_keys[4], (M, D), 1.0, 6.0, ((0, 8),)),
        "sparse_species": set_ends(skewed_ids(arg_keys[5], (M,), SPECIES, 2), jax.random.fold_in(arg_keys[5], 3), 0, SPECIES - 1).astype(jnp.int32),
    }


def reference(descriptors, env_species, structure, energies, sparse_points, sparse_species):
    scale = 1.0 / math.sqrt(D)
    weight_scale = 1.0 / math.sqrt(STRUCTS)

    def block(index):
        rows = lax.dynamic_slice_in_dim(descriptors, index * ENV_DEV, ENV_DEV, 0)
        kinds = lax.dynamic_slice_in_dim(env_species, index * ENV_DEV, ENV_DEV, 0)
        labels = lax.dynamic_index_in_dim(structure, index, 0, keepdims=False)
        dots = lax.dot_general(rows, sparse_points, (((1,), (1,)), ((), ())), preferred_element_type=jnp.float32) * scale
        squares = dots * dots
        kernel = squares * squares * (kinds[:, None] == sparse_species[None, :]).astype(jnp.float32)
        onehot = (jnp.arange(STR_DEV, dtype=jnp.int32)[:, None] == labels[None, :]).astype(jnp.float32)
        counts = lax.optimization_barrier(jnp.sum(onehot, axis=1))
        summed = jnp.dot(onehot, kernel, precision=lax.Precision.HIGHEST, preferred_element_type=jnp.float32)
        return summed * (weight_scale / counts)[:, None]
    weighted = lax.map(block, jnp.arange(N_ENV, dtype=jnp.int32)).reshape(STRUCTS, M)
    gram = lax.dot_general(weighted, weighted, (((0,), (0,)), ((), ())), precision=lax.Precision.HIGHEST, preferred_element_type=jnp.float32)
    fit_rhs = jnp.dot(energies, weighted, precision=lax.Precision.HIGHEST, preferred_element_type=jnp.float32)
    return (gram, fit_rhs)
```

```python
import math

import jax
import jax.numpy as jnp
from jax import lax
from jax.sharding import PartitionSpec as P

D = 1024
AXES = ("env", "sp")
ZL, X, C, Y, ZH = 8, 4, 2, 4, 2


def pairs(move):
    out = []
    for zl in range(ZL):
        for x in range(X):
            for c in range(C):
                for y in range(Y):
                    for zh in range(ZH):
                        a, b, d, e, f = move(zl, x, c, y, zh)
                        here = (((zl * X + x) * C + c) * Y + y) * ZH + zh
                        there = (((a * X + b) * C + d) * Y + e) * ZH + f
                        out.append((here, there))
    return out


def send(value, move):
    return lax.ppermute(value, AXES, pairs(move))


def over_z(m):
    return lambda zl, x, c, y, zh: (zl ^ m, x, c, y, zh)


def over_y(m):
    return lambda zl, x, c, y, zh: (zl, x, c, y ^ m, zh)


def over_x(m):
    return lambda zl, x, c, y, zh: (zl, x ^ m, c, y, zh)


def over_core(zl, x, c, y, zh):
    return (zl, x, 1 - c, y, zh)


def turned(flip):
    return lambda zl, x, c, y, zh: (y * ZH + zh, x, c, zl // ZH, (zl % ZH) ^ flip)


def weigh_columns(descriptors, env_kinds, points, point_kinds, onehot, factor):
    scale = 1.0 / math.sqrt(D)
    dots = (
        lax.dot_general(
            descriptors, points, (((1,), (1,)), ((), ())), preferred_element_type=jnp.float32
        )
        * scale
    )
    squares = dots * dots
    kernel = squares * squares * (env_kinds[:, None] == point_kinds[None, :]).astype(jnp.float32)
    summed = jnp.dot(
        onehot, kernel, precision=lax.Precision.HIGHEST, preferred_element_type=jnp.float32
    )
    return summed * factor[:, None]


def local(descriptors, env_species, structure, energies, sparse_points, sparse_species):
    str_local = energies.shape[0]
    cols = sparse_points.shape[0]
    total_structs = str_local * ZL * X * C
    owned = cols // (X * C)
    labels = structure[0]
    onehot = (jnp.arange(str_local, dtype=jnp.int32)[:, None] == labels[None, :]).astype(
        jnp.float32
    )
    counts = jnp.sum(onehot, axis=1)
    factor = 1.0 / math.sqrt(total_structs) / counts
    weighted = weigh_columns(
        descriptors, env_species, sparse_points, sparse_species, onehot, factor
    )
    rhs = jnp.dot(
        energies[None], weighted, precision=lax.Precision.HIGHEST, preferred_element_type=jnp.float32
    )
    env, sp = lax.axis_index("env"), lax.axis_index("sp")
    zl, c, x = env // (X * C), env % C, env // C % X

    lanes = cols // 4
    cut = weighted.reshape(str_local, 4, lanes).transpose(1, 0, 2).reshape(4 * str_local, lanes)
    tail = jnp.concatenate([rhs.reshape(4, lanes), jnp.zeros((4, lanes), jnp.float32)])
    wire = jnp.concatenate([cut, tail])

    far = send(wire, over_z(4))
    t0 = send(cut, turned(0))
    t1 = send(cut, turned(1))
    pair = jnp.stack([wire, far])
    near = [pair] + [send(pair, over_z(m)) for m in (1, 2, 3)]
    mine = jnp.stack([t0, t1])
    across = [mine] + [send(mine, over_y(m)) for m in (1, 2, 3)]

    a_blocks = jnp.stack([b[h] for h in (0, 1) for b in near])
    rhs_sum = jnp.sum(a_blocks[:, 4 * str_local : 4 * str_local + 4], axis=0).reshape(1, cols)
    b_blocks = jnp.stack([b[f] for b in across for f in (0, 1)])
    order = jnp.arange(8) ^ zl ^ sp
    b_blocks = jnp.take(b_blocks, order, axis=0)

    def rows(blocks):
        return (
            blocks[:, : 4 * str_local]
            .reshape(8, 4, str_local, lanes)
            .transpose(0, 2, 1, 3)
            .reshape(8 * str_local, cols)
        )

    tile = lax.dot_general(
        rows(b_blocks),
        rows(a_blocks),
        (((0,), (0,)), ((), ())),
        precision=lax.Precision.HIGHEST,
        preferred_element_type=jnp.float32,
    )
    tile = tile.reshape(X, C, owned, cols)
    keep = lax.dynamic_index_in_dim(tile, c, 1, keepdims=False)
    give = lax.dynamic_index_in_dim(tile, 1 - c, 1, keepdims=False)
    line = jnp.concatenate([rhs_sum, jnp.zeros((7, cols), jnp.float32)])
    payload = jnp.concatenate([give.reshape(X * owned, cols), line])
    got = send(payload, over_core)
    keep = keep + got[: X * owned].reshape(X, owned, cols)
    line = line + got[X * owned :]
    parts = [
        send(
            jnp.concatenate([lax.dynamic_index_in_dim(keep, x ^ m, 0, keepdims=False), line]),
            over_x(m),
        )
        for m in (2, 1, 3)
    ]
    total = (
        jnp.concatenate([lax.dynamic_index_in_dim(keep, x, 0, keepdims=False), line])
        + parts[0]
        + (parts[1] + parts[2])
    )
    return total[:owned].T, total[owned]


def solution(mesh):
    in_specs = (P("env", None), P("env"), P("env", None), P("env"), P("sp", None), P("sp"))
    out_specs = (P("sp", "env"), P("sp"))
    return jax.shard_map(local, mesh=mesh, in_specs=in_specs, out_specs=out_specs, check_vma=False)
```

```python
import functools
import math

import jax
import jax.numpy as jnp
from jax import lax
from jax.experimental import pallas as pl
from jax.experimental.pallas import tpu as pltpu
from jax.sharding import PartitionSpec as P

AXES = ("env", "sp")
ZL, X, C, Y, ZH = 8, 4, 2, 4, 2
KINDS = 4
LANES = 128
VMEM = pl.BlockSpec(memory_space=pltpu.VMEM)
SMEM = pl.BlockSpec(memory_space=pltpu.SMEM)
F32, BF16 = jnp.float32, jnp.bfloat16


def pairs(move):
    out = []
    for zl in range(ZL):
        for x in range(X):
            for c in range(C):
                for y in range(Y):
                    for zh in range(ZH):
                        a, b, d, e, f = move(zl, x, c, y, zh)
                        here = (((zl * X + x) * C + c) * Y + y) * ZH + zh
                        there = (((a * X + b) * C + d) * Y + e) * ZH + f
                        out.append((here, there))
    return out


def send(value, move):
    return lax.ppermute(value, AXES, pairs(move))


def over_z(m):
    return lambda zl, x, c, y, zh: (zl ^ m, x, c, y, zh)


def over_y(m):
    return lambda zl, x, c, y, zh: (zl, x, c, y ^ m, zh)


def over_x(m):
    return lambda zl, x, c, y, zh: (zl, x ^ m, c, y, zh)


def over_core(zl, x, c, y, zh):
    return (zl, x, 1 - c, y, zh)


def turned(flip):
    return lambda zl, x, c, y, zh: (y * ZH + zh, x, c, zl // ZH, (zl % ZH) ^ flip)


def halves(value):
    high = value.astype(BF16)
    return high, (value - high.astype(F32)).astype(BF16)


def weigh(steps, total, depth, desc, kinds, labels, energies, points, point_kinds, wire, acc, onehot, counts):
    step = pl.program_id(0)
    chunk, structs = desc.shape[0], energies.shape[1]

    @pl.when(step == 0)
    def _():
        own = jnp.concatenate([kinds[j : j + 1] for j in range(kinds.shape[0])], axis=1)
        code = own * structs + labels[...]
        row = lax.broadcasted_iota(jnp.int32, (KINDS * structs, code.shape[1]), 0)
        hits = (row == code).astype(F32)
        onehot[...] = hits.astype(BF16)
        counts[...] = jnp.broadcast_to(jnp.sum(hits, axis=1, keepdims=True), counts.shape)

    dots = lax.dot_general(desc[...], points[...], (((1,), (1,)), ((), ())), preferred_element_type=F32)
    squares = dots * dots
    high, low = halves(squares * squares)
    chosen = onehot[:, pl.ds(pl.multiple_of(step * chunk, chunk), chunk)]
    summed = jnp.dot(chosen, high, preferred_element_type=F32) + jnp.dot(
        chosen, low, preferred_element_type=F32
    )

    @pl.when(step == 0)
    def _():
        acc[...] = summed

    @pl.when(step > 0)
    def _():
        acc[...] += summed

    @pl.when(step == steps - 1)
    def _():
        count = sum(counts[k * structs : (k + 1) * structs, :1] for k in range(KINDS))
        factor = (1.0 / math.sqrt(total)) / count * (1.0 / float(depth) ** 2)
        mine = point_kinds[...]
        weighted = jnp.zeros((structs, acc.shape[1]), F32)
        for k in range(KINDS):
            weighted = weighted + jnp.where(mine == k, acc[k * structs : (k + 1) * structs], 0.0)
        weighted = weighted * factor
        r = lax.broadcasted_iota(jnp.int32, (structs, structs), 0)
        q = lax.broadcasted_iota(jnp.int32, (structs, structs), 1)
        column = jnp.sum(jnp.where(r == q, energies[...], 0.0), axis=1, keepdims=True)
        rhs = jnp.sum(weighted * column, axis=0, keepdims=True)
        for j in range(acc.shape[1] // LANES):
            wire[j * structs : (j + 1) * structs] = weighted[:, j * LANES : (j + 1) * LANES]
        spare = jnp.zeros((4, LANES), F32)
        wire[4 * structs :] = jnp.concatenate(
            [rhs[:, j * LANES : (j + 1) * LANES] for j in range(4)] + [spare]
        )


def weigh_call(descriptors, kinds, labels, energies, points, point_kinds, total):
    envs, depth = descriptors.shape
    cols, structs = points.shape[0], energies.shape[1]
    chunk = envs // 2
    steps = envs // chunk
    whole = lambda i: (0, 0)
    return pl.pallas_call(
        functools.partial(weigh, steps, total, depth),
        grid=(steps,),
        in_specs=[
            pl.BlockSpec((chunk, depth), lambda i: (i, 0)),
            pl.BlockSpec(kinds.shape, whole),
            pl.BlockSpec((1, envs), whole),
            pl.BlockSpec((1, structs), whole),
            pl.BlockSpec((cols, depth), whole),
            pl.BlockSpec((1, cols), whole),
        ],
        out_specs=pl.BlockSpec((4 * structs + 8, LANES), whole),
        out_shape=jax.ShapeDtypeStruct((4 * structs + 8, LANES), F32),
        scratch_shapes=[
            pltpu.VMEM((KINDS * structs, cols), F32),
            pltpu.VMEM((KINDS * structs, envs), BF16),
            pltpu.VMEM((KINDS * structs, LANES), F32),
        ],
        compiler_params=pltpu.CompilerParams(vmem_limit_bytes=56 << 20),
        cost_estimate=pl.CostEstimate(
            flops=2 * envs * depth * cols, bytes_accessed=2 * depth * (envs + cols), transcendentals=0
        ),
        name="weigh",
    )(descriptors, kinds, labels, energies, points, point_kinds)


def simple(kernel, shapes, inputs, scratch=(), flops=0, name=None, limit=8):
    moved = sum(4 * math.prod(a.shape) for a in inputs) + sum(4 * math.prod(s) for s in shapes)
    return pl.pallas_call(
        kernel,
        out_shape=[jax.ShapeDtypeStruct(s, F32) for s in shapes],
        in_specs=[SMEM if a.dtype == jnp.int32 else VMEM for a in inputs],
        out_specs=[VMEM] * len(shapes),
        scratch_shapes=list(scratch),
        compiler_params=pltpu.CompilerParams(vmem_limit_bytes=limit << 20),
        cost_estimate=pl.CostEstimate(flops=flops, bytes_accessed=moved, transcendentals=0),
        name=name,
    )(*inputs)


def pack(first, second, out):
    if len(first.shape) == 2:
        out[0], out[1] = first[...], second[...]
    else:
        half = first.shape[0]
        out[:half], out[half:] = first[...], second[...]


def join(first, second, name):
    lead = 2 if first.ndim == 2 else 2 * first.shape[0]
    (out,) = simple(pack, [(lead,) + first.shape[-2:]], [first, second], name=name)
    return out


A_ORDER = (0, 4, 2, 6, 1, 5, 3, 7)


def tile(structs, owned, where, a0, a1, b0, b1, give, keep, a_all, b_all, b_rows, product):
    cols = a_all.shape[1]
    for j in range(4):
        b_rows[j], b_rows[4 + j] = b0[j], b1[j]
    swap, core = where[0], where[1]
    rhs = jnp.zeros((8, LANES), F32)
    for p, m in enumerate(A_ORDER):
        a = (a0 if p < 4 else a1).at[p % 4]
        rhs = rhs + a[4 * structs :]
        b = b_rows.at[jnp.bitwise_xor(swap, m)]
        for j in range(cols // LANES):
            block = (pl.ds(p * structs, structs), pl.ds(j * LANES, LANES))
            a_all[block] = a[j * structs : (j + 1) * structs]
            b_all[block] = b[j * structs : (j + 1) * structs]
    a_high, a_low = halves(a_all[...])
    b_high, b_low = halves(b_all[...].T)
    product[...] = jnp.dot(b_high, a_high, preferred_element_type=F32) + (
        jnp.dot(b_high, a_low, preferred_element_type=F32)
        + jnp.dot(b_low, a_high, preferred_element_type=F32)
    )
    for x in range(X):
        here = pl.multiple_of(x * C * owned + core * owned, owned)
        there = pl.multiple_of(x * C * owned + (1 - core) * owned, owned)
        keep[x * owned : (x + 1) * owned] = product[pl.ds(here, owned)]
        give[x * owned : (x + 1) * owned] = product[pl.ds(there, owned)]
    row = lax.broadcasted_iota(jnp.int32, (8, cols), 0)
    line = jnp.concatenate([rhs[j : j + 1] for j in range(4)], axis=1)
    line = jnp.where(row == 0, line, 0.0)
    keep[X * owned :] = line
    give[X * owned :] = line


def scatter(owned, where, mine, got, stay, to1, to2, to3, total):
    total[...] = mine[...] + got[...]
    line = total[X * owned :]
    for m, out in enumerate((stay, to1, to2, to3)):
        start = pl.multiple_of(jnp.bitwise_xor(where[2], m) * owned, owned)
        out[:owned] = total[pl.ds(start, owned)]
        out[owned:] = line


def last(owned, stay, f1, f2, f3, gram, rhs):
    total = (stay[...] + f1[...]) + (f2[...] + f3[...])
    gram[...] = total[:owned]
    rhs[...] = total[owned : owned + 1]


def local(descriptors, env_species, structure, energies, sparse_points, sparse_species):
    structs, cols = energies.shape[0], sparse_points.shape[0]
    owned = cols // (X * C)
    env, sp = lax.axis_index("env"), lax.axis_index("sp")
    where = jnp.stack([(env // (X * C)) ^ sp, env % C, env // C % X]).astype(jnp.int32)

    wire = weigh_call(
        descriptors,
        env_species.reshape(-1, LANES),
        structure,
        energies[None],
        sparse_points,
        sparse_species[None],
        structs * ZL * X * C,
    )
    rows = 4 * structs
    cut = wire[:rows]
    far = send(wire, over_z(4))
    t0 = send(cut, turned(0))
    t1 = send(cut, turned(1))
    a_two = join(wire, far, "pack_a_two")
    a_got = send(a_two, over_z(2))
    b_two = join(t0, t1, "pack_b_two")
    b_got = send(b_two, over_y(1))
    a_four = join(a_two, a_got, "pack_a_four")
    a_more = send(a_four, over_z(1))
    b_four = join(b_two, b_got, "pack_b_four")
    b_more = send(b_four, over_y(2))
    half = X * owned
    give, keep = simple(
        functools.partial(tile, structs, owned),
        [(half + 8, cols)] * 2,
        [where, a_four, a_more, b_four, b_more],
        scratch=[
            pltpu.VMEM((8 * structs, cols), F32),
            pltpu.VMEM((8 * structs, cols), F32),
            pltpu.VMEM((8, rows, LANES), F32),
            pltpu.VMEM((cols, cols), F32),
        ],
        flops=6 * cols * cols * 8 * structs,
        name="tile",
        limit=16,
    )
    got = send(give, over_core)
    parts = simple(
        functools.partial(scatter, owned),
        [(owned + 8, cols)] * 4,
        [where, keep, got],
        scratch=[pltpu.VMEM((half + 8, cols), F32)],
        name="scatter",
    )
    came = [send(parts[m], over_x(m)) for m in (2, 1, 3)]
    gram, rhs = simple(
        functools.partial(last, owned), [(owned, cols), (1, cols)], [parts[0], *came], name="last"
    )
    return gram.T, rhs[0]


def solution(mesh):
    in_specs = (P("env", None), P("env"), P("env", None), P("env"), P("sp", None), P("sp"))
    out_specs = (P("sp", "env"), P("sp"))
    return jax.shard_map(local, mesh=mesh, in_specs=in_specs, out_specs=out_specs, check_vma=False)
```

```python
import functools
import math

import jax
import jax.numpy as jnp
from jax import lax
from jax.experimental import pallas as pl
from jax.experimental.pallas import tpu as pltpu
from jax.sharding import PartitionSpec as P

AXES = ("env", "sp")
ZL, X, C, Y, ZH = 8, 4, 2, 4, 2
KINDS = 4
LANES = 128
VMEM = pl.BlockSpec(memory_space=pltpu.VMEM)
SMEM = pl.BlockSpec(memory_space=pltpu.SMEM)
F32, BF16 = jnp.float32, jnp.bfloat16


def pairs(move):
    out = []
    for zl in range(ZL):
        for x in range(X):
            for c in range(C):
                for y in range(Y):
                    for zh in range(ZH):
                        a, b, d, e, f = move(zl, x, c, y, zh)
                        here = (((zl * X + x) * C + c) * Y + y) * ZH + zh
                        there = (((a * X + b) * C + d) * Y + e) * ZH + f
                        out.append((here, there))
    return out


def send(value, move):
    return lax.ppermute(value, AXES, pairs(move))


def over_z(m):
    return lambda zl, x, c, y, zh: (zl ^ m, x, c, y, zh)


def over_y(m):
    return lambda zl, x, c, y, zh: (zl, x, c, y ^ m, zh)


def over_x(m):
    return lambda zl, x, c, y, zh: (zl, x ^ m, c, y, zh)


def over_core(zl, x, c, y, zh):
    return (zl, x, 1 - c, y, zh)


def turned(flip):
    return lambda zl, x, c, y, zh: (y * ZH + zh, x, c, zl // ZH, (zl % ZH) ^ flip)


def halves(value):
    high = value.astype(BF16)
    return high, (value - high.astype(F32)).astype(BF16)


def weigh(chunks, total, desc, kinds, labels, energies, points, point_kinds, wire, cut, *scratch):
    desc_here, points_here, kinds_here, labels_here, energies_here, point_kinds_here, sems = scratch
    (envs, depth), cols, structs = desc.shape, points.shape[0], energies.shape[1]
    firsts = [sum(chunks[:i]) for i in range(len(chunks))]
    small = [
        pltpu.make_async_copy(source, target, sems.at[i])
        for i, (source, target) in enumerate(
            (
                (points, points_here),
                (kinds, kinds_here),
                (labels, labels_here),
                (energies, energies_here),
                (point_kinds, point_kinds_here),
            )
        )
    ]
    large = [
        pltpu.make_async_copy(
            desc.at[pl.ds(first, size)], desc_here.at[pl.ds(first, size)], sems.at[len(small) + i]
        )
        for i, (first, size) in enumerate(zip(firsts, chunks))
    ]
    small[0].start()
    large[0].start()
    for copy in small[1:] + large[1:]:
        copy.start()
    small[1].wait()
    small[2].wait()
    own = jnp.concatenate([kinds_here[j : j + 1] for j in range(kinds.shape[0])], axis=1)
    code = own * structs + labels_here[...]
    row = lax.broadcasted_iota(jnp.int32, (KINDS * structs, envs), 0)
    hits = (row == code).astype(F32)
    counts = jnp.sum(hits, axis=1, keepdims=True)
    onehot = hits.astype(BF16)
    small[0].wait()
    acc = jnp.zeros((KINDS * structs, cols), F32)
    for copy, first, size in zip(large, firsts, chunks):
        copy.wait()
        dots = lax.dot_general(
            desc_here[first : first + size],
            points_here[...],
            (((1,), (1,)), ((), ())),
            preferred_element_type=F32,
        )
        squares = dots * dots
        high, low = halves(squares * squares)
        chosen = onehot[:, first : first + size]
        acc = acc + (
            jnp.dot(chosen, high, preferred_element_type=F32)
            + jnp.dot(chosen, low, preferred_element_type=F32)
        )
    small[3].wait()
    small[4].wait()
    count = sum(counts[k * structs : (k + 1) * structs] for k in range(KINDS))
    factor = (1.0 / math.sqrt(total)) / count * (1.0 / float(depth) ** 2)
    mine = point_kinds_here[...]
    weighted = jnp.zeros((structs, cols), F32)
    for k in range(KINDS):
        weighted = weighted + jnp.where(mine == k, acc[k * structs : (k + 1) * structs], 0.0)
    weighted = weighted * factor
    r = lax.broadcasted_iota(jnp.int32, (structs, structs), 0)
    q = lax.broadcasted_iota(jnp.int32, (structs, structs), 1)
    column = jnp.sum(jnp.where(r == q, energies_here[...], 0.0), axis=1, keepdims=True)
    rhs = jnp.sum(weighted * column, axis=0, keepdims=True)
    for j in range(cols // LANES):
        here = slice(j * structs, (j + 1) * structs)
        wire[here] = cut[here] = weighted[:, j * LANES : (j + 1) * LANES]
    spare = jnp.zeros((4, LANES), F32)
    wire[4 * structs :] = jnp.concatenate(
        [rhs[:, j * LANES : (j + 1) * LANES] for j in range(4)] + [spare]
    )


def weigh_call(descriptors, kinds, labels, energies, points, point_kinds, total):
    envs, depth = descriptors.shape
    cols, structs = points.shape[0], energies.shape[1]
    chunks = (envs // 6, envs // 3, envs // 2)
    inputs = (descriptors, kinds, labels, energies, points, point_kinds)
    held = (descriptors, points, kinds, labels, energies, point_kinds)
    return pl.pallas_call(
        functools.partial(weigh, chunks, total),
        in_specs=[pl.BlockSpec(memory_space=pltpu.HBM)] * len(inputs),
        out_specs=[VMEM, VMEM],
        out_shape=[jax.ShapeDtypeStruct((rows, LANES), F32) for rows in (4 * structs + 8, 4 * structs)],
        scratch_shapes=[pltpu.VMEM(a.shape, a.dtype) for a in held]
        + [pltpu.SemaphoreType.DMA((5 + len(chunks),))],
        compiler_params=pltpu.CompilerParams(vmem_limit_bytes=56 << 20),
        cost_estimate=pl.CostEstimate(
            flops=2 * envs * depth * cols, bytes_accessed=2 * depth * (envs + cols), transcendentals=0
        ),
        name="weigh",
    )(*inputs)


def simple(kernel, shapes, inputs, scratch=(), flops=0, name=None, limit=8):
    moved = sum(4 * math.prod(a.shape) for a in inputs) + sum(4 * math.prod(s) for s in shapes)
    return pl.pallas_call(
        kernel,
        out_shape=[jax.ShapeDtypeStruct(s, F32) for s in shapes],
        in_specs=[SMEM if a.dtype == jnp.int32 else VMEM for a in inputs],
        out_specs=[VMEM] * len(shapes),
        scratch_shapes=list(scratch),
        compiler_params=pltpu.CompilerParams(vmem_limit_bytes=limit << 20),
        cost_estimate=pl.CostEstimate(flops=flops, bytes_accessed=moved, transcendentals=0),
        name=name,
    )(*inputs)


def pack(first, second, out):
    if len(first.shape) == 2:
        out[0], out[1] = first[...], second[...]
    else:
        half = first.shape[0]
        out[:half], out[half:] = first[...], second[...]


def join(first, second, name):
    lead = 2 if first.ndim == 2 else 2 * first.shape[0]
    (out,) = simple(pack, [(lead,) + first.shape[-2:]], [first, second], name=name)
    return out


A_ORDER = (0, 4, 2, 6, 1, 5, 3, 7)


def tile(structs, owned, where, a0, a1, b0, b1, give, keep, a_all, b_all, b_rows, product):
    cols = a_all.shape[1]
    for j in range(4):
        b_rows[j], b_rows[j ^ 6] = b0[j], b1[j]
    swap, core = where[0], where[1]
    rhs = jnp.zeros((8, LANES), F32)
    for p, m in enumerate(A_ORDER):
        a = (a0 if p < 4 else a1).at[p % 4]
        rhs = rhs + a[4 * structs :]
        b = b_rows.at[jnp.bitwise_xor(swap, m)]
        for j in range(cols // LANES):
            block = (pl.ds(p * structs, structs), pl.ds(j * LANES, LANES))
            a_all[block] = a[j * structs : (j + 1) * structs]
            b_all[block] = b[j * structs : (j + 1) * structs]
    a_high, a_low = halves(a_all[...])
    b_high, b_low = halves(b_all[...].T)
    product[...] = jnp.dot(b_high, a_high, preferred_element_type=F32) + (
        jnp.dot(b_high, a_low, preferred_element_type=F32)
        + jnp.dot(b_low, a_high, preferred_element_type=F32)
    )
    line = jnp.concatenate([rhs[:4], jnp.zeros((4, LANES), F32)])
    lanes = cols // LANES
    for half, out in ((core, keep), (1 - core, give)):
        for x in range(X):
            first = pl.multiple_of((x * C + half) * owned, owned)
            for j in range(lanes):
                out[pl.ds((x * lanes + j) * owned, owned)] = product[
                    pl.ds(first, owned), j * LANES : (j + 1) * LANES
                ]
        out[X * lanes * owned :] = line


def scatter(mine, got, out):
    piece = out.shape[1] - 8
    line = mine[X * piece :] + got[X * piece :]
    for x in range(X):
        out[x, :piece] = mine[x * piece : (x + 1) * piece] + got[x * piece : (x + 1) * piece]
        out[x, piece:] = line


def last(owned, came, gram, rhs):
    total = (came[0] + came[1]) + (came[2] + came[3])
    for j in range(gram.shape[1] // LANES):
        gram[:, j * LANES : (j + 1) * LANES] = total[j * owned : (j + 1) * owned]
    tail = total[came.shape[1] - 8 :]
    rhs[...] = jnp.concatenate([tail[j : j + 1] for j in range(4)], axis=1)


def x_groups():
    return [
        [((z * X + x) * C + c) * Y * ZH + s for x in range(X)]
        for z in range(ZL)
        for c in range(C)
        for s in range(Y * ZH)
    ]


def local(descriptors, env_species, structure, energies, sparse_points, sparse_species):
    structs, cols = energies.shape[0], sparse_points.shape[0]
    owned = cols // (X * C)
    env, sp = lax.axis_index("env"), lax.axis_index("sp")
    where = jnp.stack([(env // (X * C)) ^ sp, env % C, env // C % X]).astype(jnp.int32)

    wire, cut = weigh_call(
        descriptors,
        env_species.reshape(-1, LANES),
        structure,
        energies[None],
        sparse_points,
        sparse_species[None],
        structs * ZL * X * C,
    )
    rows = 4 * structs
    far = send(wire, over_z(4))
    t0 = send(cut, turned(0))
    t1 = send(cut, turned(1))
    a_two = join(wire, far, "pack_a_two")
    a_got = send(a_two, over_z(2))
    b_two = join(t0, t1, "pack_b_two")
    b_got = send(b_two, over_y(1))
    a_four = join(a_two, a_got, "pack_a_four")
    a_more = send(a_four, over_z(1))
    b_four = join(b_two, b_got, "pack_b_four")
    b_more = send(b_four, over_y(3))
    piece = owned * (cols // LANES)
    give, keep = simple(
        functools.partial(tile, structs, owned),
        [(X * piece + 8, LANES)] * 2,
        [where, a_four, a_more, b_four, b_more],
        scratch=[
            pltpu.VMEM((8 * structs, cols), F32),
            pltpu.VMEM((8 * structs, cols), F32),
            pltpu.VMEM((8, rows, LANES), F32),
            pltpu.VMEM((cols, cols), F32),
        ],
        flops=6 * cols * cols * 8 * structs,
        name="tile",
        limit=16,
    )
    got = send(give, over_core)
    (parts,) = simple(scatter, [(X, piece + 8, LANES)], [keep, got], name="scatter")
    came = lax.all_to_all(parts, AXES, 0, 0, axis_index_groups=x_groups())
    gram, rhs = simple(
        functools.partial(last, owned), [(owned, cols), (1, cols)], [came], name="last"
    )
    return gram.T, rhs[0]


def solution(mesh):
    in_specs = (P("env", None), P("env"), P("env", None), P("env"), P("sp", None), P("sp"))
    out_specs = (P("sp", "env"), P("sp"))
    return jax.shard_map(local, mesh=mesh, in_specs=in_specs, out_specs=out_specs, check_vma=False)
```

```python
import functools
import math

import jax
import jax.numpy as jnp
from jax import lax
from jax.experimental import pallas as pl
from jax.experimental.pallas import tpu as pltpu
from jax.sharding import PartitionSpec as P

AXES = ("env", "sp")
ZL, X, C, Y, ZH = 8, 4, 2, 4, 2
KINDS = 4
LANES = 128
VMEM = pl.BlockSpec(memory_space=pltpu.VMEM)
SMEM = pl.BlockSpec(memory_space=pltpu.SMEM)
F32, BF16 = jnp.float32, jnp.bfloat16


def pairs(move):
    out = []
    for zl in range(ZL):
        for x in range(X):
            for c in range(C):
                for y in range(Y):
                    for zh in range(ZH):
                        a, b, d, e, f = move(zl, x, c, y, zh)
                        here = (((zl * X + x) * C + c) * Y + y) * ZH + zh
                        there = (((a * X + b) * C + d) * Y + e) * ZH + f
                        out.append((here, there))
    return out


def send(value, move):
    return lax.ppermute(value, AXES, pairs(move))


def over_z(m):
    return lambda zl, x, c, y, zh: (zl ^ m, x, c, y, zh)


def over_y(m):
    return lambda zl, x, c, y, zh: (zl, x, c, y ^ m, zh)


def over_x(m):
    return lambda zl, x, c, y, zh: (zl, x ^ m, c, y, zh)


def over_core(zl, x, c, y, zh):
    return (zl, x, 1 - c, y, zh)


def turned(flip):
    return lambda zl, x, c, y, zh: (y * ZH + zh, x, c, zl // ZH, (zl % ZH) ^ flip)


def halves(value):
    high = value.astype(BF16)
    return high, (value - high.astype(F32)).astype(BF16)


def weigh(chunks, total, desc, kinds, labels, energies, points, point_kinds, wire, cut, *scratch):
    desc_here, points_here, kinds_here, labels_here, energies_here, point_kinds_here, sems = scratch
    (envs, depth), cols, structs = desc.shape, points.shape[0], energies.shape[1]
    firsts = [sum(chunks[:i]) for i in range(len(chunks))]
    small = [
        pltpu.make_async_copy(source, target, sems.at[i])
        for i, (source, target) in enumerate(
            (
                (points, points_here),
                (kinds, kinds_here),
                (labels, labels_here),
                (energies, energies_here),
                (point_kinds, point_kinds_here),
            )
        )
    ]
    large = [
        pltpu.make_async_copy(
            desc.at[pl.ds(first, size)], desc_here.at[pl.ds(first, size)], sems.at[len(small) + i]
        )
        for i, (first, size) in enumerate(zip(firsts, chunks))
    ]
    small[0].start()
    large[0].start()
    for copy in small[1:] + large[1:]:
        copy.start()
    small[1].wait()
    small[2].wait()
    own = jnp.concatenate([kinds_here[j : j + 1] for j in range(kinds.shape[0])], axis=1)
    code = own * structs + labels_here[...]
    row = lax.broadcasted_iota(jnp.int32, (KINDS * structs, envs), 0)
    hits = (row == code).astype(F32)
    counts = jnp.sum(hits, axis=1, keepdims=True)
    onehot = hits.astype(BF16)
    small[0].wait()
    acc = jnp.zeros((KINDS * structs, cols), F32)
    for copy, first, size in zip(large, firsts, chunks):
        copy.wait()
        dots = lax.dot_general(
            desc_here[first : first + size],
            points_here[...],
            (((1,), (1,)), ((), ())),
            preferred_element_type=F32,
        )
        squares = dots * dots
        high, low = halves(squares * squares)
        chosen = onehot[:, first : first + size]
        acc = acc + (
            jnp.dot(chosen, high, preferred_element_type=F32)
            + jnp.dot(chosen, low, preferred_element_type=F32)
        )
    small[3].wait()
    small[4].wait()
    count = sum(counts[k * structs : (k + 1) * structs] for k in range(KINDS))
    factor = (1.0 / math.sqrt(total)) / count * (1.0 / float(depth) ** 2)
    mine = point_kinds_here[...]
    weighted = jnp.zeros((structs, cols), F32)
    for k in range(KINDS):
        weighted = weighted + jnp.where(mine == k, acc[k * structs : (k + 1) * structs], 0.0)
    weighted = weighted * factor
    r = lax.broadcasted_iota(jnp.int32, (structs, structs), 0)
    q = lax.broadcasted_iota(jnp.int32, (structs, structs), 1)
    column = jnp.sum(jnp.where(r == q, energies_here[...], 0.0), axis=1, keepdims=True)
    rhs = jnp.sum(weighted * column, axis=0, keepdims=True)
    for j in range(cols // LANES):
        here = slice(j * structs, (j + 1) * structs)
        wire[here] = cut[here] = weighted[:, j * LANES : (j + 1) * LANES]
    spare = jnp.zeros((4, LANES), F32)
    wire[4 * structs :] = jnp.concatenate(
        [rhs[:, j * LANES : (j + 1) * LANES] for j in range(4)] + [spare]
    )


def weigh_call(descriptors, kinds, labels, energies, points, point_kinds, total):
    envs, depth = descriptors.shape
    cols, structs = points.shape[0], energies.shape[1]
    chunks = (envs // 6, envs // 3, envs // 2)
    inputs = (descriptors, kinds, labels, energies, points, point_kinds)
    held = (descriptors, points, kinds, labels, energies, point_kinds)
    return pl.pallas_call(
        functools.partial(weigh, chunks, total),
        in_specs=[pl.BlockSpec(memory_space=pltpu.HBM)] * len(inputs),
        out_specs=[VMEM, VMEM],
        out_shape=[jax.ShapeDtypeStruct((rows, LANES), F32) for rows in (4 * structs + 8, 4 * structs)],
        scratch_shapes=[pltpu.VMEM(a.shape, a.dtype) for a in held]
        + [pltpu.SemaphoreType.DMA((5 + len(chunks),))],
        compiler_params=pltpu.CompilerParams(vmem_limit_bytes=56 << 20),
        cost_estimate=pl.CostEstimate(
            flops=2 * envs * depth * cols, bytes_accessed=2 * depth * (envs + cols), transcendentals=0
        ),
        name="weigh",
    )(*inputs)


def simple(kernel, shapes, inputs, scratch=(), flops=0, name=None, limit=8):
    moved = sum(4 * math.prod(a.shape) for a in inputs) + sum(4 * math.prod(s) for s in shapes)
    return pl.pallas_call(
        kernel,
        out_shape=[jax.ShapeDtypeStruct(s, F32) for s in shapes],
        in_specs=[SMEM if a.dtype == jnp.int32 else VMEM for a in inputs],
        out_specs=[VMEM] * len(shapes),
        scratch_shapes=list(scratch),
        compiler_params=pltpu.CompilerParams(vmem_limit_bytes=limit << 20),
        cost_estimate=pl.CostEstimate(flops=flops, bytes_accessed=moved, transcendentals=0),
        name=name,
    )(*inputs)


def pack(first, second, out):
    if len(first.shape) == 2:
        out[0], out[1] = first[...], second[...]
    else:
        half = first.shape[0]
        out[:half], out[half:] = first[...], second[...]


def join(first, second, name):
    lead = 2 if first.ndim == 2 else 2 * first.shape[0]
    (out,) = simple(pack, [(lead,) + first.shape[-2:]], [first, second], name=name)
    return out


A_ORDER = (0, 4, 2, 6, 1, 5, 3, 7)


def tile(structs, owned, where, a0, a1, b_lanes, give, keep, a_all, b_all, b_rows, product):
    cols = a_all.shape[1]
    for j in range(Y):
        b_rows[2 * j], b_rows[2 * j + 1] = b_lanes[j, 0], b_lanes[j, 1]
    k, zh, core = where[0], where[1], where[2]
    rhs = jnp.zeros((8, LANES), F32)
    for p, m in enumerate(A_ORDER):
        a = (a0 if p < 4 else a1).at[p % 4]
        rhs = rhs + a[4 * structs :]
        b = b_rows.at[(k ^ m) ^ zh]
        for j in range(cols // LANES):
            block = (pl.ds(p * structs, structs), pl.ds(j * LANES, LANES))
            a_all[block] = a[j * structs : (j + 1) * structs]
            b_all[block] = b[j * structs : (j + 1) * structs]
    a_high, a_low = halves(a_all[...])
    b_high, b_low = halves(b_all[...].T)
    product[...] = jnp.dot(b_high, a_high, preferred_element_type=F32) + (
        jnp.dot(b_high, a_low, preferred_element_type=F32)
        + jnp.dot(b_low, a_high, preferred_element_type=F32)
    )
    line = jnp.concatenate([rhs[:4], jnp.zeros((4, LANES), F32)])
    lanes = cols // LANES
    for half, out in ((core, keep), (1 - core, give)):
        for x in range(X):
            first = pl.multiple_of((x * C + half) * owned, owned)
            for j in range(lanes):
                out[pl.ds((x * lanes + j) * owned, owned)] = product[
                    pl.ds(first, owned), j * LANES : (j + 1) * LANES
                ]
        out[X * lanes * owned :] = line


def scatter(mine, got, out):
    piece = out.shape[1] - 8
    line = mine[X * piece :] + got[X * piece :]
    for x in range(X):
        out[x, :piece] = mine[x * piece : (x + 1) * piece] + got[x * piece : (x + 1) * piece]
        out[x, piece:] = line


def last(owned, came, gram, rhs):
    total = (came[0] + came[1]) + (came[2] + came[3])
    for j in range(gram.shape[1] // LANES):
        gram[:, j * LANES : (j + 1) * LANES] = total[j * owned : (j + 1) * owned]
    tail = total[came.shape[1] - 8 :]
    rhs[...] = jnp.concatenate([tail[j : j + 1] for j in range(4)], axis=1)


def repeat(first, second, out):
    for j in range(Y):
        out[j, 0], out[j, 1] = first[...], second[...]


def y_groups():
    return [[e * Y * ZH + y * ZH + h for y in range(Y)] for e in range(ZL * X * C) for h in range(ZH)]


def x_groups():
    return [
        [((z * X + x) * C + c) * Y * ZH + s for x in range(X)]
        for z in range(ZL)
        for c in range(C)
        for s in range(Y * ZH)
    ]


def local(descriptors, env_species, structure, energies, sparse_points, sparse_species):
    structs, cols = energies.shape[0], sparse_points.shape[0]
    owned = cols // (X * C)
    env, sp = lax.axis_index("env"), lax.axis_index("sp")
    where = jnp.stack([env // (X * C), sp % ZH, env % C]).astype(jnp.int32)

    wire, cut = weigh_call(
        descriptors,
        env_species.reshape(-1, LANES),
        structure,
        energies[None],
        sparse_points,
        sparse_species[None],
        structs * ZL * X * C,
    )
    rows = 4 * structs
    far = send(wire, over_z(4))
    t0 = send(cut, turned(0))
    t1 = send(cut, turned(1))
    a_two = join(wire, far, "pack_a_two")
    a_got = send(a_two, over_z(2))
    (b_own,) = simple(repeat, [(Y, 2, rows, LANES)], [t0, t1], name="repeat")
    b_all = lax.all_to_all(b_own, AXES, 0, 0, axis_index_groups=y_groups())
    a_four = join(a_two, a_got, "pack_a_four")
    a_more = send(a_four, over_z(1))
    piece = owned * (cols // LANES)
    give, keep = simple(
        functools.partial(tile, structs, owned),
        [(X * piece + 8, LANES)] * 2,
        [where, a_four, a_more, b_all],
        scratch=[
            pltpu.VMEM((8 * structs, cols), F32),
            pltpu.VMEM((8 * structs, cols), F32),
            pltpu.VMEM((8, rows, LANES), F32),
            pltpu.VMEM((cols, cols), F32),
        ],
        flops=6 * cols * cols * 8 * structs,
        name="tile",
        limit=16,
    )
    got = send(give, over_core)
    (parts,) = simple(scatter, [(X, piece + 8, LANES)], [keep, got], name="scatter")
    came = lax.all_to_all(parts, AXES, 0, 0, axis_index_groups=x_groups())
    gram, rhs = simple(
        functools.partial(last, owned), [(owned, cols), (1, cols)], [came], name="last"
    )
    return gram.T, rhs[0]


def solution(mesh):
    in_specs = (P("env", None), P("env"), P("env", None), P("env"), P("sp", None), P("sp"))
    out_specs = (P("sp", "env"), P("sp"))
    return jax.shard_map(local, mesh=mesh, in_specs=in_specs, out_specs=out_specs, check_vma=False)
```

```python
import functools
import math

import jax
import jax.numpy as jnp
from jax import lax
from jax.experimental import pallas as pl
from jax.experimental.pallas import tpu as pltpu
from jax.sharding import PartitionSpec as P

AXES = ("env", "sp")
ZL, X, C, Y, ZH = 8, 4, 2, 4, 2
KINDS = 4
LANES = 128
VMEM = pl.BlockSpec(memory_space=pltpu.VMEM)
SMEM = pl.BlockSpec(memory_space=pltpu.SMEM)
F32, BF16 = jnp.float32, jnp.bfloat16


def pairs(move):
    out = []
    for zl in range(ZL):
        for x in range(X):
            for c in range(C):
                for y in range(Y):
                    for zh in range(ZH):
                        a, b, d, e, f = move(zl, x, c, y, zh)
                        here = (((zl * X + x) * C + c) * Y + y) * ZH + zh
                        there = (((a * X + b) * C + d) * Y + e) * ZH + f
                        out.append((here, there))
    return out


def send(value, move):
    return lax.ppermute(value, AXES, pairs(move))


def over_z(m):
    return lambda zl, x, c, y, zh: (zl ^ m, x, c, y, zh)


def over_y(m):
    return lambda zl, x, c, y, zh: (zl, x, c, y ^ m, zh)


def over_x(m):
    return lambda zl, x, c, y, zh: (zl, x ^ m, c, y, zh)


def over_core(zl, x, c, y, zh):
    return (zl, x, 1 - c, y, zh)


def nearer(k, q):
    return (k - q > 2) | ((k - q == 2) & (k < Y))


def turned(flip):
    def move(zl, x, c, y, zh):
        k, q, upper = y * ZH + zh, zl % Y, zl // Y
        return (k, x, c, q, zh ^ upper ^ flip ^ int(nearer(k, q)))

    return move


def halves(value):
    high = value.astype(BF16)
    return high, (value - high.astype(F32)).astype(BF16)


def weigh(chunks, total, desc, kinds, labels, energies, points, point_kinds, wire, cut, *scratch):
    desc_here, points_here, kinds_here, labels_here, energies_here, point_kinds_here, sems = scratch
    (envs, depth), cols, structs = desc.shape, points.shape[0], energies.shape[1]
    firsts = [sum(chunks[:i]) for i in range(len(chunks))]
    small = [
        pltpu.make_async_copy(source, target, sems.at[i])
        for i, (source, target) in enumerate(
            (
                (points, points_here),
                (kinds, kinds_here),
                (labels, labels_here),
                (energies, energies_here),
                (point_kinds, point_kinds_here),
            )
        )
    ]
    large = [
        pltpu.make_async_copy(
            desc.at[pl.ds(first, size)], desc_here.at[pl.ds(first, size)], sems.at[len(small) + i]
        )
        for i, (first, size) in enumerate(zip(firsts, chunks))
    ]
    small[0].start()
    large[0].start()
    for copy in small[1:] + large[1:]:
        copy.start()
    small[1].wait()
    small[2].wait()
    own = jnp.concatenate([kinds_here[j : j + 1] for j in range(kinds.shape[0])], axis=1)
    code = own * structs + labels_here[...]
    row = lax.broadcasted_iota(jnp.int32, (KINDS * structs, envs), 0)
    hits = (row == code).astype(F32)
    counts = jnp.sum(hits, axis=1, keepdims=True)
    onehot = hits.astype(BF16)
    small[0].wait()
    acc = jnp.zeros((KINDS * structs, cols), F32)
    for copy, first, size in zip(large, firsts, chunks):
        copy.wait()
        dots = lax.dot_general(
            desc_here[first : first + size],
            points_here[...],
            (((1,), (1,)), ((), ())),
            preferred_element_type=F32,
        )
        squares = dots * dots
        high, low = halves(squares * squares)
        chosen = onehot[:, first : first + size]
        acc = acc + (
            jnp.dot(chosen, high, preferred_element_type=F32)
            + jnp.dot(chosen, low, preferred_element_type=F32)
        )
    small[3].wait()
    small[4].wait()
    count = sum(counts[k * structs : (k + 1) * structs] for k in range(KINDS))
    factor = (1.0 / math.sqrt(total)) / count * (1.0 / float(depth) ** 2)
    mine = point_kinds_here[...]
    weighted = jnp.zeros((structs, cols), F32)
    for k in range(KINDS):
        weighted = weighted + jnp.where(mine == k, acc[k * structs : (k + 1) * structs], 0.0)
    weighted = weighted * factor
    r = lax.broadcasted_iota(jnp.int32, (structs, structs), 0)
    q = lax.broadcasted_iota(jnp.int32, (structs, structs), 1)
    column = jnp.sum(jnp.where(r == q, energies_here[...], 0.0), axis=1, keepdims=True)
    rhs = jnp.sum(weighted * column, axis=0, keepdims=True)
    for j in range(cols // LANES):
        here = slice(j * structs, (j + 1) * structs)
        wire[here] = cut[here] = weighted[:, j * LANES : (j + 1) * LANES]
    spare = jnp.zeros((4, LANES), F32)
    wire[4 * structs :] = jnp.concatenate(
        [rhs[:, j * LANES : (j + 1) * LANES] for j in range(4)] + [spare]
    )


def weigh_call(descriptors, kinds, labels, energies, points, point_kinds, total):
    envs, depth = descriptors.shape
    cols, structs = points.shape[0], energies.shape[1]
    chunks = (envs // 6, envs // 3, envs // 2)
    inputs = (descriptors, kinds, labels, energies, points, point_kinds)
    held = (descriptors, points, kinds, labels, energies, point_kinds)
    return pl.pallas_call(
        functools.partial(weigh, chunks, total),
        in_specs=[pl.BlockSpec(memory_space=pltpu.HBM)] * len(inputs),
        out_specs=[VMEM, VMEM],
        out_shape=[jax.ShapeDtypeStruct((rows, LANES), F32) for rows in (4 * structs + 8, 4 * structs)],
        scratch_shapes=[pltpu.VMEM(a.shape, a.dtype) for a in held]
        + [pltpu.SemaphoreType.DMA((5 + len(chunks),))],
        compiler_params=pltpu.CompilerParams(vmem_limit_bytes=56 << 20),
        cost_estimate=pl.CostEstimate(
            flops=2 * envs * depth * cols, bytes_accessed=2 * depth * (envs + cols), transcendentals=0
        ),
        name="weigh",
    )(*inputs)


def simple(kernel, shapes, inputs, scratch=(), flops=0, name=None, limit=8):
    moved = sum(4 * math.prod(a.shape) for a in inputs) + sum(4 * math.prod(s) for s in shapes)
    return pl.pallas_call(
        kernel,
        out_shape=[jax.ShapeDtypeStruct(s, F32) for s in shapes],
        in_specs=[SMEM if a.dtype == jnp.int32 else VMEM for a in inputs],
        out_specs=[VMEM] * len(shapes),
        scratch_shapes=list(scratch),
        compiler_params=pltpu.CompilerParams(vmem_limit_bytes=limit << 20),
        cost_estimate=pl.CostEstimate(flops=flops, bytes_accessed=moved, transcendentals=0),
        name=name,
    )(*inputs)


def pack(first, second, out):
    if len(first.shape) == 2:
        out[0], out[1] = first[...], second[...]
    else:
        half = first.shape[0]
        out[:half], out[half:] = first[...], second[...]


def join(first, second, name):
    lead = 2 if first.ndim == 2 else 2 * first.shape[0]
    (out,) = simple(pack, [(lead,) + first.shape[-2:]], [first, second], name=name)
    return out


A_ORDER = (0, 4, 2, 6, 1, 5, 3, 7)


def tile(structs, owned, where, a0, a1, b_lanes, give, keep, a_all, b_all, b_rows, product):
    cols = a_all.shape[1]
    for j in range(Y):
        b_rows[2 * j], b_rows[2 * j + 1] = b_lanes[j, 0], b_lanes[j, 1]
    k, zh, core = where[0], where[1], where[2]
    rhs = jnp.zeros((8, LANES), F32)
    for p, m in enumerate(A_ORDER):
        a = (a0 if p < 4 else a1).at[p % 4]
        rhs = rhs + a[4 * structs :]
        lane = (k ^ m) & (Y - 1)
        slot = ((k ^ m) // Y) ^ zh ^ (k & 1) ^ nearer(k, lane).astype(jnp.int32)
        b = b_rows.at[2 * lane + slot]
        for j in range(cols // LANES):
            block = (pl.ds(p * structs, structs), pl.ds(j * LANES, LANES))
            a_all[block] = a[j * structs : (j + 1) * structs]
            b_all[block] = b[j * structs : (j + 1) * structs]
    a_high, a_low = halves(a_all[...])
    b_high, b_low = halves(b_all[...].T)
    product[...] = jnp.dot(b_high, a_high, preferred_element_type=F32) + (
        jnp.dot(b_high, a_low, preferred_element_type=F32)
        + jnp.dot(b_low, a_high, preferred_element_type=F32)
    )
    line = jnp.concatenate([rhs[:4], jnp.zeros((4, LANES), F32)])
    lanes = cols // LANES
    for half, out in ((core, keep), (1 - core, give)):
        for x in range(X):
            first = pl.multiple_of((x * C + half) * owned, owned)
            for j in range(lanes):
                out[pl.ds((x * lanes + j) * owned, owned)] = product[
                    pl.ds(first, owned), j * LANES : (j + 1) * LANES
                ]
        out[X * lanes * owned :] = line


def scatter(mine, got, out):
    piece = out.shape[1] - 8
    line = mine[X * piece :] + got[X * piece :]
    for x in range(X):
        out[x, :piece] = mine[x * piece : (x + 1) * piece] + got[x * piece : (x + 1) * piece]
        out[x, piece:] = line


def last(owned, came, gram, rhs):
    total = (came[0] + came[1]) + (came[2] + came[3])
    for j in range(gram.shape[1] // LANES):
        gram[:, j * LANES : (j + 1) * LANES] = total[j * owned : (j + 1) * owned]
    tail = total[came.shape[1] - 8 :]
    rhs[...] = jnp.concatenate([tail[j : j + 1] for j in range(4)], axis=1)


def repeat(first, second, out):
    for j in range(Y):
        out[j, 0], out[j, 1] = first[...], second[...]


def y_groups():
    return [[e * Y * ZH + y * ZH + h for y in range(Y)] for e in range(ZL * X * C) for h in range(ZH)]


def x_groups():
    return [
        [((z * X + x) * C + c) * Y * ZH + s for x in range(X)]
        for z in range(ZL)
        for c in range(C)
        for s in range(Y * ZH)
    ]


def local(descriptors, env_species, structure, energies, sparse_points, sparse_species):
    structs, cols = energies.shape[0], sparse_points.shape[0]
    owned = cols // (X * C)
    env, sp = lax.axis_index("env"), lax.axis_index("sp")
    where = jnp.stack([env // (X * C), sp % ZH, env % C]).astype(jnp.int32)

    wire, cut = weigh_call(
        descriptors,
        env_species.reshape(-1, LANES),
        structure,
        energies[None],
        sparse_points,
        sparse_species[None],
        structs * ZL * X * C,
    )
    rows = 4 * structs
    far = send(wire, over_z(4))
    t0 = send(cut, turned(0))
    t1 = send(cut, turned(1))
    a_two = join(wire, far, "pack_a_two")
    a_got = send(a_two, over_z(2))
    (b_own,) = simple(repeat, [(Y, 2, rows, LANES)], [t0, t1], name="repeat")
    b_all = lax.all_to_all(b_own, AXES, 0, 0, axis_index_groups=y_groups())
    a_four = join(a_two, a_got, "pack_a_four")
    a_more = send(a_four, over_z(1))
    piece = owned * (cols // LANES)
    give, keep = simple(
        functools.partial(tile, structs, owned),
        [(X * piece + 8, LANES)] * 2,
        [where, a_four, a_more, b_all],
        scratch=[
            pltpu.VMEM((8 * structs, cols), F32),
            pltpu.VMEM((8 * structs, cols), F32),
            pltpu.VMEM((8, rows, LANES), F32),
            pltpu.VMEM((cols, cols), F32),
        ],
        flops=6 * cols * cols * 8 * structs,
        name="tile",
        limit=16,
    )
    got = send(give, over_core)
    (parts,) = simple(scatter, [(X, piece + 8, LANES)], [keep, got], name="scatter")
    came = lax.all_to_all(parts, AXES, 0, 0, axis_index_groups=x_groups())
    gram, rhs = simple(
        functools.partial(last, owned), [(owned, cols), (1, cols)], [came], name="last"
    )
    return gram.T, rhs[0]


def solution(mesh):
    in_specs = (P("env", None), P("env"), P("env", None), P("env"), P("sp", None), P("sp"))
    out_specs = (P("sp", "env"), P("sp"))
    return jax.shard_map(local, mesh=mesh, in_specs=in_specs, out_specs=out_specs, check_vma=False)
```

```python
import functools
import math

import jax
import jax.numpy as jnp
from jax import lax
from jax.experimental import pallas as pl
from jax.experimental.pallas import tpu as pltpu
from jax.sharding import PartitionSpec as P

AXES = ("env", "sp")
ZL, X, C, Y, ZH = 8, 4, 2, 4, 2
KINDS = 4
LANES = 128
VMEM = pl.BlockSpec(memory_space=pltpu.VMEM)
SMEM = pl.BlockSpec(memory_space=pltpu.SMEM)
F32, BF16 = jnp.float32, jnp.bfloat16


def pairs(move):
    out = []
    for zl in range(ZL):
        for x in range(X):
            for c in range(C):
                for y in range(Y):
                    for zh in range(ZH):
                        a, b, d, e, f = move(zl, x, c, y, zh)
                        here = (((zl * X + x) * C + c) * Y + y) * ZH + zh
                        there = (((a * X + b) * C + d) * Y + e) * ZH + f
                        out.append((here, there))
    return out


def send(value, move):
    return lax.ppermute(value, AXES, pairs(move))


def over_z(m):
    return lambda zl, x, c, y, zh: (zl ^ m, x, c, y, zh)


def over_y(m):
    return lambda zl, x, c, y, zh: (zl, x, c, y ^ m, zh)


def over_x(m):
    return lambda zl, x, c, y, zh: (zl, x ^ m, c, y, zh)


def over_core(zl, x, c, y, zh):
    return (zl, x, 1 - c, y, zh)


def nearer(k, q):
    return (k - q > 2) | ((k - q == 2) & (k < Y))


def turned(flip):
    def move(zl, x, c, y, zh):
        k, q, upper = y * ZH + zh, zl % Y, zl // Y
        return (k, x, c, q, zh ^ upper ^ flip ^ int(nearer(k, q)))

    return move


def halves(value):
    high = value.astype(BF16)
    return high, (value - high.astype(F32)).astype(BF16)


def weigh(chunks, total, desc, kinds, labels, energies, points, point_kinds, wire, cut, *scratch):
    desc_here, points_here, kinds_here, labels_here, energies_here, point_kinds_here, sems = scratch
    (envs, depth), cols, structs = desc.shape, points.shape[0], energies.shape[1]
    firsts = [sum(chunks[:i]) for i in range(len(chunks))]
    small = [
        pltpu.make_async_copy(source, target, sems.at[i])
        for i, (source, target) in enumerate(
            (
                (points, points_here),
                (kinds, kinds_here),
                (labels, labels_here),
                (energies, energies_here),
                (point_kinds, point_kinds_here),
            )
        )
    ]
    large = [
        pltpu.make_async_copy(
            desc.at[pl.ds(first, size)], desc_here.at[pl.ds(first, size)], sems.at[len(small) + i]
        )
        for i, (first, size) in enumerate(zip(firsts, chunks))
    ]
    for copy in (small[1], small[2], small[0], large[0], *large[1:], *small[3:]):
        copy.start()
    small[1].wait()
    small[2].wait()
    own = jnp.concatenate([kinds_here[j : j + 1] for j in range(kinds.shape[0])], axis=1)
    code = own * structs + labels_here[...]
    row = lax.broadcasted_iota(jnp.int32, (KINDS * structs, envs), 0)
    hits = (row == code).astype(F32)
    counts = jnp.sum(hits, axis=1, keepdims=True)
    onehot = hits.astype(BF16)
    small[0].wait()
    acc = jnp.zeros((KINDS * structs, cols), F32)
    for copy, first, size in zip(large, firsts, chunks):
        copy.wait()
        dots = lax.dot_general(
            desc_here[first : first + size],
            points_here[...],
            (((1,), (1,)), ((), ())),
            preferred_element_type=F32,
        )
        squares = dots * dots
        high, low = halves(squares * squares)
        chosen = onehot[:, first : first + size]
        acc = acc + (
            jnp.dot(chosen, high, preferred_element_type=F32)
            + jnp.dot(chosen, low, preferred_element_type=F32)
        )
    small[3].wait()
    small[4].wait()
    count = sum(counts[k * structs : (k + 1) * structs] for k in range(KINDS))
    factor = (1.0 / math.sqrt(total)) / count * (1.0 / float(depth) ** 2)
    mine = point_kinds_here[...]
    weighted = jnp.zeros((structs, cols), F32)
    for k in range(KINDS):
        weighted = weighted + jnp.where(mine == k, acc[k * structs : (k + 1) * structs], 0.0)
    weighted = weighted * factor
    r = lax.broadcasted_iota(jnp.int32, (structs, structs), 0)
    q = lax.broadcasted_iota(jnp.int32, (structs, structs), 1)
    column = jnp.sum(jnp.where(r == q, energies_here[...], 0.0), axis=1, keepdims=True)
    rhs = jnp.sum(weighted * column, axis=0, keepdims=True)
    for j in range(cols // LANES):
        here = slice(j * structs, (j + 1) * structs)
        wire[here] = cut[here] = weighted[:, j * LANES : (j + 1) * LANES]
    spare = jnp.zeros((4, LANES), F32)
    wire[4 * structs :] = jnp.concatenate(
        [rhs[:, j * LANES : (j + 1) * LANES] for j in range(4)] + [spare]
    )


def weigh_call(descriptors, kinds, labels, energies, points, point_kinds, total):
    envs, depth = descriptors.shape
    cols, structs = points.shape[0], energies.shape[1]
    chunks = (envs // 6, envs // 3, envs // 2)
    inputs = (descriptors, kinds, labels, energies, points, point_kinds)
    held = (descriptors, points, kinds, labels, energies, point_kinds)
    return pl.pallas_call(
        functools.partial(weigh, chunks, total),
        in_specs=[pl.BlockSpec(memory_space=pltpu.HBM)] * len(inputs),
        out_specs=[VMEM, VMEM],
        out_shape=[jax.ShapeDtypeStruct((rows, LANES), F32) for rows in (4 * structs + 8, 4 * structs)],
        scratch_shapes=[pltpu.VMEM(a.shape, a.dtype) for a in held]
        + [pltpu.SemaphoreType.DMA((5 + len(chunks),))],
        compiler_params=pltpu.CompilerParams(vmem_limit_bytes=56 << 20),
        cost_estimate=pl.CostEstimate(
            flops=2 * envs * depth * cols, bytes_accessed=2 * depth * (envs + cols), transcendentals=0
        ),
        name="weigh",
    )(*inputs)


def simple(kernel, shapes, inputs, scratch=(), flops=0, name=None, limit=8):
    moved = sum(4 * math.prod(a.shape) for a in inputs) + sum(4 * math.prod(s) for s in shapes)
    return pl.pallas_call(
        kernel,
        out_shape=[jax.ShapeDtypeStruct(s, F32) for s in shapes],
        in_specs=[SMEM if a.dtype == jnp.int32 else VMEM for a in inputs],
        out_specs=[VMEM] * len(shapes),
        scratch_shapes=list(scratch),
        compiler_params=pltpu.CompilerParams(vmem_limit_bytes=limit << 20),
        cost_estimate=pl.CostEstimate(flops=flops, bytes_accessed=moved, transcendentals=0),
        name=name,
    )(*inputs)


def pack(first, second, out):
    if len(first.shape) == 2:
        out[0], out[1] = first[...], second[...]
    else:
        half = first.shape[0]
        out[:half], out[half:] = first[...], second[...]


def join(first, second, name):
    lead = 2 if first.ndim == 2 else 2 * first.shape[0]
    (out,) = simple(pack, [(lead,) + first.shape[-2:]], [first, second], name=name)
    return out


A_ORDER = (0, 4, 2, 6, 1, 5, 3, 7)


def tile(structs, owned, where, a0, a1, b_lanes, give, keep, a_all, b_all, b_rows, product):
    cols = a_all.shape[1]
    for j in range(Y):
        b_rows[2 * j], b_rows[2 * j + 1] = b_lanes[j, 0], b_lanes[j, 1]
    k, zh, core = where[0], where[1], where[2]
    rhs = jnp.zeros((8, LANES), F32)
    for p, m in enumerate(A_ORDER):
        a = (a0 if p < 4 else a1).at[p % 4]
        rhs = rhs + a[4 * structs :]
        lane = (k ^ m) & (Y - 1)
        slot = ((k ^ m) // Y) ^ zh ^ (k & 1) ^ nearer(k, lane).astype(jnp.int32)
        b = b_rows.at[2 * lane + slot]
        for j in range(cols // LANES):
            block = (pl.ds(p * structs, structs), pl.ds(j * LANES, LANES))
            a_all[block] = a[j * structs : (j + 1) * structs]
            b_all[block] = b[j * structs : (j + 1) * structs]
    a_high, a_low = halves(a_all[...])
    b_high, b_low = halves(b_all[...].T)
    product[...] = jnp.dot(b_high, a_high, preferred_element_type=F32) + (
        jnp.dot(b_high, a_low, preferred_element_type=F32)
        + jnp.dot(b_low, a_high, preferred_element_type=F32)
    )
    line = jnp.concatenate([rhs[:4], jnp.zeros((4, LANES), F32)])
    lanes = cols // LANES
    for half, out in ((core, keep), (1 - core, give)):
        for x in range(X):
            first = pl.multiple_of((x * C + half) * owned, owned)
            for j in range(lanes):
                out[pl.ds((x * lanes + j) * owned, owned)] = product[
                    pl.ds(first, owned), j * LANES : (j + 1) * LANES
                ]
        out[X * lanes * owned :] = line


def scatter(mine, got, out):
    piece = out.shape[1] - 8
    line = mine[X * piece :] + got[X * piece :]
    for x in range(X):
        out[x, :piece] = mine[x * piece : (x + 1) * piece] + got[x * piece : (x + 1) * piece]
        out[x, piece:] = line


def last(owned, came, gram, rhs):
    total = (came[0] + came[1]) + (came[2] + came[3])
    for j in range(gram.shape[1] // LANES):
        gram[:, j * LANES : (j + 1) * LANES] = total[j * owned : (j + 1) * owned]
    tail = total[came.shape[1] - 8 :]
    rhs[...] = jnp.concatenate([tail[j : j + 1] for j in range(4)], axis=1)


def repeat(first, second, out):
    for j in range(Y):
        out[j, 0], out[j, 1] = first[...], second[...]


def y_groups():
    return [[e * Y * ZH + y * ZH + h for y in range(Y)] for e in range(ZL * X * C) for h in range(ZH)]


def x_groups():
    return [
        [((z * X + x) * C + c) * Y * ZH + s for x in range(X)]
        for z in range(ZL)
        for c in range(C)
        for s in range(Y * ZH)
    ]


def local(descriptors, env_species, structure, energies, sparse_points, sparse_species):
    structs, cols = energies.shape[0], sparse_points.shape[0]
    owned = cols // (X * C)
    env, sp = lax.axis_index("env"), lax.axis_index("sp")
    where = jnp.stack([env // (X * C), sp % ZH, env % C]).astype(jnp.int32)

    wire, cut = weigh_call(
        descriptors,
        env_species.reshape(-1, LANES),
        structure,
        energies[None],
        sparse_points,
        sparse_species[None],
        structs * ZL * X * C,
    )
    rows = 4 * structs
    far = send(wire, over_z(4))
    t0 = send(cut, turned(0))
    t1 = send(cut, turned(1))
    a_two = join(wire, far, "pack_a_two")
    a_got = send(a_two, over_z(2))
    (b_own,) = simple(repeat, [(Y, 2, rows, LANES)], [t0, t1], name="repeat")
    b_all = lax.all_to_all(b_own, AXES, 0, 0, axis_index_groups=y_groups())
    a_four = join(a_two, a_got, "pack_a_four")
    a_more = send(a_four, over_z(1))
    piece = owned * (cols // LANES)
    give, keep = simple(
        functools.partial(tile, structs, owned),
        [(X * piece + 8, LANES)] * 2,
        [where, a_four, a_more, b_all],
        scratch=[
            pltpu.VMEM((8 * structs, cols), F32),
            pltpu.VMEM((8 * structs, cols), F32),
            pltpu.VMEM((8, rows, LANES), F32),
            pltpu.VMEM((cols, cols), F32),
        ],
        flops=6 * cols * cols * 8 * structs,
        name="tile",
        limit=16,
    )
    got = send(give, over_core)
    (parts,) = simple(scatter, [(X, piece + 8, LANES)], [keep, got], name="scatter")
    came = lax.all_to_all(parts, AXES, 0, 0, axis_index_groups=x_groups())
    gram, rhs = simple(
        functools.partial(last, owned), [(owned, cols), (1, cols)], [came], name="last"
    )
    return gram.T, rhs[0]


def solution(mesh):
    in_specs = (P("env", None), P("env"), P("env", None), P("env"), P("sp", None), P("sp"))
    out_specs = (P("sp", "env"), P("sp"))
    return jax.shard_map(local, mesh=mesh, in_specs=in_specs, out_specs=out_specs, check_vma=False)
```
